512 devices in a mesh: grp: 8 (over y, x_hi), blk: 64 (over z, x_lo, core).
Axes of the slice: x: 4 (x_hi: 2, x_lo: 2; x = x_hi * 2 + x_lo), y: 4, z: 16, core: 2. Of those that a mesh axis runs over, the one named last changes fastest.
Arguments:
- query_out: bfloat16 [64, 14336], P('blk', 'grp'), may hold values from -6 to 6
- query_in: bfloat16 [64, 8192], P('blk', 'grp'), may hold values from -6 to 6
- basis_out: float32 [14336, 14336], P('grp', 'blk'), may hold values from -0.046875 to 0.046875
- basis_in: float32 [8192, 8192], P('grp', 'blk'), may hold values from -0.0625 to 0.0625
- eigen_out: float32 [14336], replicated, may hold values from 0.05 to 20
- eigen_in: float32 [8192], replicated, may hold values from 0.05 to 20
- panel_index: int32 [2, 64], replicated, may hold values from 0 to 63, each once within a row
- train_out: bfloat16 [32768, 14336], P(('grp', 'blk')), may hold values from -0.046875 to 0.046875
- train_in: bfloat16 [32768, 8192], P(('grp', 'blk')), may hold values from -0.0625 to 0.0625
- train_count: int32 [512], P(('grp', 'blk')), may hold values from 1 to 2, as said below
Outputs:
- scores: float32 [1024, 2], P(('grp', 'blk'))
The draws below stay inside these ranges and needn't reach their ends.
Inputs may be any that keep to these rules, and one draw needn't show every extreme that they name: Each device's count of live training slots; the first train_count[d] of its 2 slots are live.
All inputs are finite; a program needn't handle non-finite values.
Results may differ from the reference program's by a relative error of at most 0.0003.
Values may be sent and summed in bfloat16 or wider, within the bound.
No kernel may reach another device: no remote copies, remote signals or barrier semaphores. Data moves between devices by JAX's collectives and lax.ppermute only.
A program may use at most 64 MiB of HBM per device.

```python
import math
import jax
import jax.numpy as jnp
from jax import lax

DOUT = 14336
DIN = 8192
RANK = 32
NQ = 2
SEQ_DEV = 2
QROWS = 64
TRAIN = 1024
N_BLK = 64


def draw_train_count(key, part):
    devices_total = TRAIN // SEQ_DEV
    heavy_draw = jax.random.randint(key, (devices_total,), 0, 4)
    counts = jnp.where(heavy_draw == 0, SEQ_DEV, 1).astype(jnp.int32)
    heavy_slot = jax.random.randint(jax.random.fold_in(key, 1), (), 0, devices_total)
    light_slot = (heavy_slot + 1 + jax.random.randint(jax.random.fold_in(key, 2), (), 0, devices_total - 1)) % devices_total
    counts = counts.at[heavy_slot].set(SEQ_DEV).at[light_slot].set(1)
    return counts.astype(jnp.int32)


def levels(own_key, extent, cuts, least, top_value):
    def one(position, shards_of):
        steps = jax.random.uniform(jax.random.fold_in(jax.random.fold_in(own_key, 6), position), (shards_of,), jnp.float32, least / len(cuts), top_value / len(cuts))
        return jnp.repeat(jnp.exp(steps), extent[position] // shards_of).reshape((-1,) + (1,) * (len(extent) - position - 1))

    factor_of = one(*cuts[0])
    for cut in cuts[1:]:
        factor_of = factor_of * one(*cut)
    return factor_of


def gaussian(rng, dims, spread, bound, split=(), kind=jnp.bfloat16):
    drawn = spread * jax.random.normal(rng, dims, jnp.float32)
    if split:
        drawn = drawn * levels(rng, dims, split, -0.22, 0.18)
    return jnp.clip(drawn, -bound, bound).astype(kind)


def setup_inputs(seed: int = 0) -> dict:
    arg_keys = jax.random.split(jax.random.key(seed), 11)
    query_out = gaussian(arg_keys[0], (QROWS, DOUT), 1.0, 6.0, ((0, 64), (1, 8)))
    query_in = gaussian(arg_keys[1], (QROWS, DIN), 1.0, 6.0, ((0, 64), (1, 8)))
    basis_out = gaussian(arg_keys[2], (DOUT, DOUT), DOUT ** -0.5, 0.046875, ((0, 8), (1, 64)), jnp.float32)
    basis_in = gaussian(arg_keys[3], (DIN, DIN), DIN ** -0.5, 0.0625, ((0, 8), (1, 64)), jnp.float32)
    eigen_out = jnp.clip(jnp.exp(jax.random.uniform(arg_keys[4], (DOUT,), jnp.float32, math.log(0.05), math.log(20.0))), 0.05, 20.0)
    eigen_in = jnp.clip(jnp.exp(jax.random.uniform(arg_keys[5], (DIN,), jnp.float32, math.log(0.05), math.log(20.0))), 0.05, 20.0)
    panel_index = jax.vmap(lambda own: jax.random.permutation(own, N_BLK))(jax.random.split(arg_keys[6], 2)).reshape((2, N_BLK)).astype(jnp.int32)
    train_out = gaussian(arg_keys[7], (TRAIN * RANK, DOUT), DOUT ** -0.5, 0.046875, ((0, 512),))
    train_in = gaussian(arg_keys[8], (TRAIN * RANK, DIN), DIN ** -0.5, 0.0625, ((0, 512),))
    train_count = draw_train_count(jax.random.fold_in(arg_keys[10], 71), 0)
    return dict(query_out=query_out, query_in=query_in, basis_out=basis_out, basis_in=basis_in, eigen_out=eigen_out, eigen_in=eigen_in, panel_index=panel_index, train_out=train_out, train_in=train_in, train_count=train_count)


damping = 0.5


def precondition(queries, basis_full, eigen_values, panel_order):
    panel_width = basis_full.shape[1] // N_BLK
    damped_scale = (1.0 / (eigen_values + damping)).reshape(N_BLK, panel_width)[panel_order].reshape(-1)
    rotated = jnp.dot(queries.astype(jnp.float32), basis_full, precision=lax.Precision.HIGHEST, preferred_element_type=jnp.float32)
    restored = jnp.dot(rotated * damped_scale[None, :], basis_full.T, precision=lax.Precision.HIGHEST, preferred_element_type=jnp.float32)
    return restored


def reference(query_out, query_in, basis_out, basis_in, eigen_out, eigen_in, panel_index, train_out, train_in, train_count):
    pre_out = precondition(query_out, basis_out, eigen_out, panel_index[0])
    pre_in = precondition(query_in, basis_in, eigen_in, panel_index[1])
    along_out = jnp.dot(train_out.astype(jnp.float32), pre_out.T, precision=lax.Precision.HIGHEST, preferred_element_type=jnp.float32)
    along_in = jnp.dot(train_in.astype(jnp.float32), pre_in.T, precision=lax.Precision.HIGHEST, preferred_element_type=jnp.float32)
    product = (along_out * along_in).reshape(TRAIN, RANK, NQ, RANK)
    scores = jnp.sum(product, axis=(1, 3)) / RANK
    slot_ids = jnp.arange(TRAIN, dtype=jnp.int32)
    live = (slot_ids % SEQ_DEV) < jnp.repeat(train_count, SEQ_DEV)
    return jnp.where(live[:, None], scores, 0.0).astype(jnp.float32)
```

```python
import functools

import jax
import jax.numpy as jnp
from jax import lax
from jax.experimental import pallas as pl
from jax.experimental.pallas import tpu as pltpu
from jax.sharding import Mesh
from jax.sharding import PartitionSpec as P

NQ = 2
SEQ_DEV = 2
RANK = 32
DAMPING = 0.5
LANES = 128
SLOTS = 24
STEPS = 8
TOP = 32766.0
GRP = ("y", "xh")
BLK = ("z", "xl", "c")
VMEM_LIMIT = 48 * 1024 * 1024

f32 = jnp.float32
bf16 = jnp.bfloat16


def split2(x):
    hi = x.astype(bf16)
    return hi, (x - hi.astype(f32)).astype(bf16)


def dot_nn(a, b):
    return lax.dot_general(a, b, (((1,), (0,)), ((), ())), preferred_element_type=f32)


def dot_nt(a, b):
    return lax.dot_general(a, b, (((1,), (1,)), ((), ())), preferred_element_type=f32)


def call(body, out_shape, scratch=(), n_in=1, smem=()):
    specs = [
        pl.BlockSpec(memory_space=pltpu.SMEM if i in smem else pltpu.VMEM) for i in range(n_in)
    ]
    outs = jax.tree.map(lambda _: pl.BlockSpec(memory_space=pltpu.VMEM), out_shape)
    return pl.pallas_call(
        body,
        out_shape=out_shape,
        in_specs=specs,
        out_specs=outs,
        scratch_shapes=list(scratch),
        compiler_params=pltpu.CompilerParams(vmem_limit_bytes=VMEM_LIMIT),
    )


def rotate_body(n_out, n_in, q_ref, bto_ref, bi_ref, part_ref, wide, rows):
    n = q_ref.shape[0]
    wide[...] = q_ref[...].astype(f32).reshape(wide.shape)
    for r in range(n_out + n_in):
        rows[:, r * LANES : (r + 1) * LANES] = wide[pl.ds(r, n, stride=SLOTS), :].astype(bf16)
    w_out = bto_ref.shape[0]
    q_out = rows[:, : n_out * LANES]
    q_in = rows[:, n_out * LANES :]
    hi, lo = split2(bto_ref[...])
    part_ref[...] = jnp.zeros_like(part_ref)
    part_ref[:, :w_out] = dot_nt(q_out, hi) + dot_nt(q_out, lo)
    hi, lo = split2(bi_ref[...])
    part_ref[:, part_ref.shape[1] - bi_ref.shape[1] :] = dot_nn(q_in, hi) + dot_nn(q_in, lo)


def restore_body(core_ref, part_ref, scale_ref, bto_ref, bi_ref, keep_ref, send_ref, coords):
    total = part_ref[0]
    for g in range(1, part_ref.shape[0]):
        total = total + part_ref[g]
    coords[...] = total * scale_ref[...]
    half = keep_ref.shape[0]
    core = core_ref[0]
    mine = coords[pl.ds(pl.multiple_of(core * half, half), half), :]
    other = coords[pl.ds(pl.multiple_of((1 - core) * half, half), half), :]
    both = jnp.concatenate([mine, other], axis=0)
    w_out, k_out = bto_ref.shape
    w_in = bi_ref.shape[1]
    hi, lo = split2(both[:, :w_out])
    b_hi, b_lo = split2(bto_ref[...])
    term = dot_nn(hi, b_hi) + dot_nn(hi, b_lo) + dot_nn(lo, b_hi)
    keep_ref[:, :k_out] = term[:half]
    send_ref[:, :k_out] = term[half:]
    hi, lo = split2(both[:, both.shape[1] - w_in :])
    b_hi, b_lo = split2(bi_ref[...])
    term = dot_nt(hi, b_hi) + dot_nt(hi, b_lo) + dot_nt(lo, b_hi)
    keep_ref[:, k_out:] = term[:half]
    send_ref[:, k_out:] = term[half:]


def level(top):
    return jnp.ceil(STEPS * jnp.log2(jnp.maximum(top, 1e-30)))


def unit(steps):
    return jnp.exp2(steps * (1.0 / STEPS)) * (1.0 / TOP)


def encode_rows_body(n_out, n_in, keep_ref, got_ref, code_ref, wide):
    n = keep_ref.shape[0]
    for first, count, row in ((0, n_out, n_out + n_in), (n_out, n_in, n_out + n_in + 1)):
        x = (
            keep_ref[:, first * LANES : (first + count) * LANES]
            + got_ref[:, first * LANES : (first + count) * LANES]
        )
        steps = level(jnp.max(jnp.abs(x), axis=1, keepdims=True))
        codes = jnp.round(x * (1.0 / unit(steps)))
        for r in range(count):
            wide[pl.ds(first + r, n, stride=SLOTS), :] = codes[:, r * LANES : (r + 1) * LANES]
        wide[pl.ds(row, n, stride=SLOTS), :] = jnp.broadcast_to(steps, (n, LANES))
    code_ref[...] = wide[...].astype(jnp.int32).astype(jnp.int16).reshape(code_ref.shape)


def sum_codes_body(n_out, n_in, code_ref, out_ref):
    slot = lax.broadcasted_iota(jnp.int32, (SLOTS, LANES), 0)
    is_out = slot < n_out
    is_in = jnp.logical_and(slot >= n_out, slot < n_out + n_in)
    total = jnp.zeros((SLOTS, LANES), f32)
    for j in range(code_ref.shape[0]):
        x = code_ref[j].astype(jnp.int32).astype(f32)
        a = x[n_out + n_in : n_out + n_in + 1]
        b = x[n_out + n_in + 1 : n_out + n_in + 2]
        total = total + x * unit(jnp.where(is_out, a, b))
    size = jnp.abs(total)
    steps_out = level(jnp.max(jnp.where(is_out, size, 0.0), keepdims=True))
    steps_in = level(jnp.max(jnp.where(is_in, size, 0.0), keepdims=True))
    steps = jnp.where(is_out, steps_out, steps_in)
    codes = jnp.round(total * (1.0 / unit(steps)))
    codes = jnp.where(slot == n_out + n_in, steps_out, codes)
    codes = jnp.where(slot == n_out + n_in + 1, steps_in, codes)
    codes = codes.astype(jnp.int32).astype(jnp.int16)
    for j in range(out_ref.shape[0]):
        out_ref[j] = codes


def score_body(n_out, n_in, groups, live_ref, code_ref, to_ref, ti_ref, out_ref, wide, hi, lo):
    n = code_ref.shape[0] // groups
    along_out = jnp.zeros((to_ref.shape[0], n), f32)
    along_in = jnp.zeros((ti_ref.shape[0], n), f32)
    for g in range(groups):
        x = code_ref[g * n : (g + 1) * n].astype(jnp.int32).astype(f32)
        wide[...] = x.reshape(wide.shape)
        for first, count, row in ((0, n_out, n_out + n_in), (n_out, n_in, n_out + n_in + 1)):
            scale = unit(wide[pl.ds(row, n, stride=SLOTS), :])
            for r in range(count):
                v = wide[pl.ds(first + r, n, stride=SLOTS), :] * scale
                a, b = split2(v)
                hi[:, r * LANES : (r + 1) * LANES] = a
                lo[:, r * LANES : (r + 1) * LANES] = b
            width = count * LANES
            t_ref = to_ref if first == 0 else ti_ref
            t = t_ref[:, g * width : (g + 1) * width]
            part = dot_nt(t, hi[:, :width]) + dot_nt(t, lo[:, :width])
            if first == 0:
                along_out = along_out + part
            else:
                along_in = along_in + part
    product = along_out * along_in
    rows = product.shape[0]
    q_id = lax.rem(lax.broadcasted_iota(jnp.int32, (rows, n), 1), 16) // 8
    s_id = lax.broadcasted_iota(jnp.int32, (rows, n), 0) // RANK
    row = lax.broadcasted_iota(jnp.int32, out_ref.shape, 0)
    col = lax.broadcasted_iota(jnp.int32, out_ref.shape, 1)
    result = jnp.zeros(out_ref.shape, f32)
    for s in range(SEQ_DEV):
        for q in range(NQ):
            picked = jnp.where(jnp.logical_and(s_id == s, q_id == q), product, 0.0)
            value = jnp.sum(picked) * (1.0 / RANK)
            value = jnp.where(live_ref[0] > s, value, 0.0)
            result = jnp.where(jnp.logical_and(row == s, col == q), value, result)
    out_ref[...] = result


def panel_scale(eigen_values, panel, width):
    picked = lax.dynamic_slice_in_dim(eigen_values, panel * width, width)
    return 1.0 / (picked + DAMPING)


def per_device(qo, qi, bo, bi, eo, ei, panels, to, ti, live):
    n_out, n_in = qo.shape[1] // LANES, qi.shape[1] // LANES
    data = n_out + n_in
    nz, nxl, nc = (lax.axis_size(a) for a in BLK)
    n_grp = lax.axis_size(GRP)
    n_rows = nz * nxl * nc
    half = n_rows // nc
    position = lax.axis_index(BLK)
    w_out, w_in = bo.shape[1], bi.shape[1]
    w_pad = -(-w_out // LANES) * LANES
    bto = bo.T

    own = jnp.concatenate([qo, qi], axis=1).reshape(data, LANES)
    own = jnp.pad(own, ((0, SLOTS - data), (0, 0)))
    spread = jnp.broadcast_to(own[None], (nz * nxl, SLOTS, LANES))
    got = lax.all_to_all(spread, ("z", "xl"), split_axis=0, concat_axis=0, tiled=True)
    queries = lax.all_gather(got, "c", axis=0, tiled=True)

    part = call(
        functools.partial(rotate_body, n_out, n_in),
        jax.ShapeDtypeStruct((n_rows, w_pad + w_in), f32),
        [pltpu.VMEM((n_rows * SLOTS, LANES), f32), pltpu.VMEM((n_rows, data * LANES), bf16)],
        n_in=3,
    )(queries, bto, bi)
    parts = lax.all_to_all(
        jnp.broadcast_to(part[None], (n_grp, *part.shape)), GRP, split_axis=0, concat_axis=0
    )

    scale = jnp.concatenate(
        [
            panel_scale(eo, panels[0, position], w_out),
            jnp.zeros((w_pad - w_out,), f32),
            panel_scale(ei, panels[1, position], w_in),
        ]
    )[None]
    core = lax.axis_index("c").astype(jnp.int32)[None]
    block = jax.ShapeDtypeStruct((half, data * LANES), f32)
    keep, send = call(
        restore_body,
        (block, block),
        [pltpu.VMEM((n_rows, w_pad + w_in), f32)],
        n_in=5,
        smem=(0,),
    )(core, parts, scale, bto, bi)
    other = lax.ppermute(send, "c", [(0, 1), (1, 0)])
    codes = call(
        functools.partial(encode_rows_body, n_out, n_in),
        jax.ShapeDtypeStruct((half, SLOTS, LANES), jnp.int16),
        [pltpu.VMEM((half * SLOTS, LANES), f32)],
        n_in=2,
    )(keep, other)
    codes = lax.all_to_all(codes, ("z", "xl"), split_axis=0, concat_axis=0, tiled=True)
    codes = call(
        functools.partial(sum_codes_body, n_out, n_in),
        jax.ShapeDtypeStruct((nz, SLOTS, LANES), jnp.int16),
    )(codes)
    codes = lax.all_to_all(codes, "z", split_axis=0, concat_axis=0, tiled=True)
    codes = lax.all_gather(codes, ("y", "xh", "xl", "c"), axis=0, tiled=True)
    return call(
        functools.partial(score_body, n_out, n_in, n_grp),
        jax.ShapeDtypeStruct((SEQ_DEV, NQ), f32),
        [
            pltpu.VMEM((n_rows * SLOTS, LANES), f32),
            pltpu.VMEM((n_rows, n_out * LANES), bf16),
            pltpu.VMEM((n_rows, n_out * LANES), bf16),
        ],
        n_in=4,
        smem=(0,),
    )(live, codes, to, ti)


def solution(mesh):
    fine = Mesh(mesh.devices.reshape(4, 2, 16, 2, 2), GRP + BLK)
    in_specs = (
        P(BLK, GRP),
        P(BLK, GRP),
        P(GRP, BLK),
        P(GRP, BLK),
        P(),
        P(),
        P(),
        P(GRP + BLK, None),
        P(GRP + BLK, None),
        P(GRP + BLK),
    )
    out_specs = P(GRP + BLK, None)
    return jax.shard_map(
        per_device, mesh=fine, in_specs=in_specs, out_specs=out_specs, check_vma=False
    )
```

```python
import functools

import jax
import jax.numpy as jnp
from jax import lax
from jax.experimental import pallas as pl
from jax.experimental.pallas import tpu as pltpu
from jax.sharding import Mesh
from jax.sharding import PartitionSpec as P

NQ = 2
SEQ_DEV = 2
RANK = 32
DAMPING = 0.5
LANES = 128
SLOTS = 24
STEPS = 8
TOP = 32766.0
OWN_FLOPS = 20_000_000_000
PAD = 32
GRP = ("y", "xh")
BLK = ("z", "xl", "c")
VMEM_LIMIT = 12 * 1024 * 1024

f32 = jnp.float32
bf16 = jnp.bfloat16


def split2(x):
    hi = x.astype(bf16)
    return hi, (x - hi.astype(f32)).astype(bf16)


def dot_nn(a, b):
    return lax.dot_general(a, b, (((1,), (0,)), ((), ())), preferred_element_type=f32)


def dot_nt(a, b):
    return lax.dot_general(a, b, (((1,), (1,)), ((), ())), preferred_element_type=f32)


def call(body, out_shape, scratch=(), n_in=1, smem=(), flops=0):
    specs = [
        pl.BlockSpec(memory_space=pltpu.SMEM if i in smem else pltpu.VMEM) for i in range(n_in)
    ]
    outs = jax.tree.map(lambda _: pl.BlockSpec(memory_space=pltpu.VMEM), out_shape)
    return pl.pallas_call(
        body,
        out_shape=out_shape,
        in_specs=specs,
        out_specs=outs,
        scratch_shapes=list(scratch),
        cost_estimate=pl.CostEstimate(flops=flops, bytes_accessed=0, transcendentals=0)
        if flops
        else None,
        compiler_params=pltpu.CompilerParams(vmem_limit_bytes=VMEM_LIMIT),
    )


def level(top):
    return jnp.ceil(STEPS * jnp.log2(jnp.maximum(top, 1e-30)))


def unit(steps):
    return jnp.exp2(steps * (1.0 / STEPS)) * (1.0 / TOP)


def to_code(x):
    return x.astype(jnp.int32).astype(jnp.int16)


def from_code(x):
    return x.astype(jnp.int32).astype(f32)


def split_body(bto_ref, bi_ref, out_ref):
    w_out, k_out = bto_ref.shape
    k_in = bi_ref.shape[0]
    rest = jnp.zeros((out_ref.shape[1] - w_out, k_out - k_in), bf16)
    for part, (b_out, b_in) in enumerate(zip(split2(bto_ref[...]), split2(bi_ref[...].T))):
        out_ref[part, :w_out, :] = b_out
        out_ref[part, w_out:, :k_in] = b_in
        out_ref[part, w_out:, k_in:] = rest


def rotate(rows, b_ref, w_out, k_out, k_in):
    n = rows.shape[0]
    w_pad = w_out + PAD
    lane = lax.broadcasted_iota(jnp.int32, (n, w_pad), 1)
    q_out, q_in = rows[:, :k_out], rows[:, k_out:]
    out = dot_nt(q_out, b_ref[0, :w_pad, :]) + dot_nt(q_out, b_ref[1, :w_pad, :])
    out = jnp.where(lane < w_out, out, 0.0)
    inn = dot_nt(q_in, b_ref[0, w_out:, :k_in]) + dot_nt(q_in, b_ref[1, w_out:, :k_in])
    s_out = level(jnp.max(jnp.abs(out), axis=1, keepdims=True))
    s_in = level(jnp.max(jnp.abs(inn), axis=1, keepdims=True))
    out = jnp.round(out * (1.0 / unit(s_out)))
    out = jnp.where(lane < w_out, out, jnp.where(lane < w_out + PAD // 2, s_out, s_in))
    inn = jnp.round(inn * (1.0 / unit(s_in)))
    return to_code(out), to_code(inn)


def rotate_own_body(n_out, n_in, w_out, q_ref, b_ref, rows_ref, code_ref, wide):
    n = q_ref.shape[0]
    wide[...] = q_ref[...].astype(f32).reshape(wide.shape)
    for r in range(n_out + n_in):
        rows_ref[:, r * LANES : (r + 1) * LANES] = wide[pl.ds(r, n, stride=SLOTS), :].astype(bf16)
    out, inn = rotate(rows_ref, b_ref, w_out, n_out * LANES, n_in * LANES)
    code_ref[:, : w_out + PAD] = out
    code_ref[:, w_out + PAD :] = inn


def rotate_mate_body(n_out, n_in, w_out, rows_ref, b_ref, code_ref, part_ref):
    out, inn = rotate(rows_ref, b_ref, w_out, n_out * LANES, n_in * LANES)
    w_all = code_ref.shape[1]
    for g in range(part_ref.shape[0]):
        part_ref[g, :, :w_all] = code_ref[...]
        part_ref[g, :, w_all : w_all + w_out + PAD] = out
        part_ref[g, :, w_all + w_out + PAD :] = inn


def panel_scales(spot, w_out, panel_ref, eo_ref, ei_ref):
    start = panel_ref[0, spot] * w_out
    row, shift = start // LANES, start % LANES
    last = eo_ref.shape[0] - 1
    spans = -(-w_out // LANES) + 1
    held = jnp.concatenate(
        [eo_ref[pl.ds(jnp.minimum(row + i, last), 1), :] for i in range(spans)], axis=1
    )
    picked = held[:, : w_out + PAD]
    for by in range(PAD, LANES, PAD):
        picked = jnp.where(shift == by, held[:, by : by + w_out + PAD], picked)
    e_in = ei_ref[pl.ds(panel_ref[1, spot], 1), :]
    return 1.0 / (picked + DAMPING), 1.0 / (e_in + DAMPING)


def restore_body(
    n_out, n_in, w_out, at_ref, panel_ref, part_ref, eo_ref, ei_ref, own_ref, mate_ref, code_ref, wide
):
    n = part_ref.shape[1]
    k_out, k_in = n_out * LANES, n_in * LANES
    w_in = own_ref.shape[1] - w_out
    w_pad = w_out + PAD
    w_all = w_pad + w_in
    lane = lax.broadcasted_iota(jnp.int32, (n, w_pad), 1)
    x_out = jnp.zeros((n, k_out), f32)
    x_in = jnp.zeros((n, k_in), f32)
    for k, b_ref in enumerate((own_ref, mate_ref)):
        at = k * w_all
        t_out = jnp.zeros((n, w_pad), f32)
        t_in = jnp.zeros((n, w_in), f32)
        for g in range(part_ref.shape[0]):
            x = from_code(part_ref[g, :, at : at + w_all])
            t_out += x[:, :w_pad] * unit(x[:, w_out : w_out + 1])
            t_in += x[:, w_pad:] * unit(x[:, w_out + PAD // 2 : w_out + PAD // 2 + 1])
        s_out, s_in = panel_scales(at_ref[k], w_out, panel_ref, eo_ref, ei_ref)
        t_out = jnp.where(lane < w_out, t_out * s_out, 0.0)
        both = jnp.concatenate(split2(t_out), axis=0)
        x = dot_nn(both, b_ref[0, :w_pad, :])
        x_out += x[:n] + x[n:] + dot_nn(both[:n], b_ref[1, :w_pad, :])
        both = jnp.concatenate(split2(t_in * s_in), axis=0)
        x = dot_nn(both, b_ref[0, w_out:, :k_in])
        x_in += x[:n] + x[n:] + dot_nn(both[:n], b_ref[1, w_out:, :k_in])
    for first, x, row in ((0, x_out, n_out + n_in), (n_out, x_in, n_out + n_in + 1)):
        steps = level(jnp.max(jnp.abs(x), axis=1, keepdims=True))
        codes = jnp.round(x * (1.0 / unit(steps)))
        for r in range(x.shape[1] // LANES):
            wide[pl.ds(first + r, n, stride=SLOTS), :] = codes[:, r * LANES : (r + 1) * LANES]
        wide[pl.ds(row, n, stride=SLOTS), :] = jnp.broadcast_to(steps, (n, LANES))
    code_ref[...] = to_code(wide[...]).reshape(code_ref.shape)


def sum_codes_body(n_out, n_in, code_ref, out_ref):
    slot = lax.broadcasted_iota(jnp.int32, (SLOTS, LANES), 0)
    is_out = slot < n_out
    is_in = jnp.logical_and(slot >= n_out, slot < n_out + n_in)
    total = jnp.zeros((SLOTS, LANES), f32)
    for j in range(code_ref.shape[0]):
        x = from_code(code_ref[j])
        a = x[n_out + n_in : n_out + n_in + 1]
        b = x[n_out + n_in + 1 : n_out + n_in + 2]
        total = total + x * unit(jnp.where(is_out, a, b))
    size = jnp.abs(total)
    steps_out = level(jnp.max(jnp.where(is_out, size, 0.0), keepdims=True))
    steps_in = level(jnp.max(jnp.where(is_in, size, 0.0), keepdims=True))
    steps = jnp.where(is_out, steps_out, steps_in)
    codes = jnp.round(total * (1.0 / unit(steps)))
    codes = jnp.where(slot == n_out + n_in, steps_out, codes)
    codes = jnp.where(slot == n_out + n_in + 1, steps_in, codes)
    codes = to_code(codes)
    for j in range(out_ref.shape[0]):
        out_ref[j] = codes


def score_body(n_out, n_in, groups, live_ref, code_ref, to_ref, ti_ref, out_ref, wide, hi, lo):
    n = code_ref.shape[0] // groups
    along_out = jnp.zeros((to_ref.shape[0], n), f32)
    along_in = jnp.zeros((ti_ref.shape[0], n), f32)
    for g in range(groups):
        x = from_code(code_ref[g * n : (g + 1) * n])
        wide[...] = x.reshape(wide.shape)
        for first, count, row in ((0, n_out, n_out + n_in), (n_out, n_in, n_out + n_in + 1)):
            scale = unit(wide[pl.ds(row, n, stride=SLOTS), :])
            for r in range(count):
                v = wide[pl.ds(first + r, n, stride=SLOTS), :] * scale
                a, b = split2(v)
                hi[:, r * LANES : (r + 1) * LANES] = a
                lo[:, r * LANES : (r + 1) * LANES] = b
            width = count * LANES
            t_ref = to_ref if first == 0 else ti_ref
            t = t_ref[:, g * width : (g + 1) * width]
            part = dot_nt(t, hi[:, :width]) + dot_nt(t, lo[:, :width])
            if first == 0:
                along_out = along_out + part
            else:
                along_in = along_in + part
    product = along_out * along_in
    rows = product.shape[0]
    q_id = lax.rem(lax.broadcasted_iota(jnp.int32, (rows, n), 1), 16) // 8
    s_id = lax.broadcasted_iota(jnp.int32, (rows, n), 0) // RANK
    row = lax.broadcasted_iota(jnp.int32, out_ref.shape, 0)
    col = lax.broadcasted_iota(jnp.int32, out_ref.shape, 1)
    result = jnp.zeros(out_ref.shape, f32)
    for s in range(SEQ_DEV):
        for q in range(NQ):
            picked = jnp.where(jnp.logical_and(s_id == s, q_id == q), product, 0.0)
            value = jnp.sum(picked) * (1.0 / RANK)
            value = jnp.where(live_ref[0] > s, value, 0.0)
            result = jnp.where(jnp.logical_and(row == s, col == q), value, result)
    out_ref[...] = result


def spread(x, axes):
    n = lax.axis_size(axes)
    x = jnp.broadcast_to(x[None], (n, *x.shape))
    return lax.all_to_all(x, axes, split_axis=0, concat_axis=0, tiled=True)


def per_device(qo, qi, bo, bi, eo, ei, panels, to, ti, live):
    n_out, n_in = qo.shape[1] // LANES, qi.shape[1] // LANES
    data = n_out + n_in
    nz, nxl, nc = (lax.axis_size(a) for a in BLK)
    n_grp = lax.axis_size(GRP)
    half = nz * nxl
    n_rows = half * nc
    position = lax.axis_index(BLK)
    w_out, w_in = bo.shape[1], bi.shape[1]
    w_all = w_out + PAD + w_in

    own_q = jnp.concatenate([qo, qi], axis=1).reshape(data, LANES)
    own_q = jnp.pad(own_q, ((0, SLOTS - data), (0, 0)))
    queries = spread(own_q, ("z", "xl"))

    own = call(
        split_body, jax.ShapeDtypeStruct((2, w_out + w_in, bo.shape[0]), bf16), n_in=2
    )(bo.T, bi)
    mate = lax.ppermute(own, "c", [(0, 1), (1, 0)])
    rows, own_part = call(
        functools.partial(rotate_own_body, n_out, n_in, w_out),
        (
            jax.ShapeDtypeStruct((half, data * LANES), bf16),
            jax.ShapeDtypeStruct((half, w_all), jnp.int16),
        ),
        [pltpu.VMEM((half * SLOTS, LANES), f32)],
        n_in=2,
        flops=OWN_FLOPS,
    )(queries, own)
    part = call(
        functools.partial(rotate_mate_body, n_out, n_in, w_out),
        jax.ShapeDtypeStruct((n_grp, half, nc * w_all), jnp.int16),
        n_in=3,
    )(rows, mate, own_part)
    parts = lax.all_to_all(part, GRP, split_axis=0, concat_axis=0, tiled=True)

    mate_spot = position + 1 - 2 * lax.axis_index("c")
    spots = jnp.stack([position, mate_spot]).astype(jnp.int32)
    codes = call(
        functools.partial(restore_body, n_out, n_in, w_out),
        jax.ShapeDtypeStruct((half, SLOTS, LANES), jnp.int16),
        [pltpu.VMEM((half * SLOTS, LANES), f32)],
        n_in=7,
        smem=(0, 1),
    )(spots, panels, parts, eo.reshape(-1, LANES), ei.reshape(-1, w_in), own, mate)
    codes = lax.all_to_all(codes, ("z", "xl"), split_axis=0, concat_axis=0, tiled=True)
    codes = call(
        functools.partial(sum_codes_body, n_out, n_in),
        jax.ShapeDtypeStruct((nz, SLOTS, LANES), jnp.int16),
    )(codes)
    codes = lax.all_to_all(codes, "z", split_axis=0, concat_axis=0, tiled=True)
    codes = lax.all_gather(codes, ("y", "xh", "xl", "c"), axis=0, tiled=True)
    return call(
        functools.partial(score_body, n_out, n_in, n_grp),
        jax.ShapeDtypeStruct((SEQ_DEV, NQ), f32),
        [
            pltpu.VMEM((n_rows * SLOTS, LANES), f32),
            pltpu.VMEM((n_rows, n_out * LANES), bf16),
            pltpu.VMEM((n_rows, n_out * LANES), bf16),
        ],
        n_in=4,
        smem=(0,),
    )(live, codes, to, ti)


def solution(mesh):
    fine = Mesh(mesh.devices.reshape(4, 2, 16, 2, 2), GRP + BLK)
    in_specs = (
        P(BLK, GRP),
        P(BLK, GRP),
        P(GRP, BLK),
        P(GRP, BLK),
        P(),
        P(),
        P(),
        P(GRP + BLK, None),
        P(GRP + BLK, None),
        P(GRP + BLK),
    )
    out_specs = P(GRP + BLK, None)
    return jax.shard_map(
        per_device, mesh=fine, in_specs=in_specs, out_specs=out_specs, check_vma=False
    )
```

```python
import functools

import jax
import jax.numpy as jnp
from jax import lax
from jax.experimental import pallas as pl
from jax.experimental.pallas import tpu as pltpu
from jax.sharding import Mesh
from jax.sharding import PartitionSpec as P

NQ = 2
SEQ_DEV = 2
RANK = 32
DAMPING = 0.5
LANES = 128
SLOTS = 24
STEPS = 8
TOP = 32766.0
OWN_FLOPS = 20_000_000_000
PAD = 32
GRP = ("y", "xh")
BLK = ("z", "xl", "c")
VMEM_LIMIT = 12 * 1024 * 1024

f32 = jnp.float32
bf16 = jnp.bfloat16


def split2(x):
    hi = x.astype(bf16)
    return hi, (x - hi.astype(f32)).astype(bf16)


def dot_nn(a, b):
    return lax.dot_general(a, b, (((1,), (0,)), ((), ())), preferred_element_type=f32)


def dot_nt(a, b):
    return lax.dot_general(a, b, (((1,), (1,)), ((), ())), preferred_element_type=f32)


def call(body, out_shape, scratch=(), n_in=1, smem=(), flops=0):
    specs = [
        pl.BlockSpec(memory_space=pltpu.SMEM if i in smem else pltpu.VMEM) for i in range(n_in)
    ]
    outs = jax.tree.map(lambda _: pl.BlockSpec(memory_space=pltpu.VMEM), out_shape)
    return pl.pallas_call(
        body,
        out_shape=out_shape,
        in_specs=specs,
        out_specs=outs,
        scratch_shapes=list(scratch),
        cost_estimate=pl.CostEstimate(flops=flops, bytes_accessed=0, transcendentals=0)
        if flops
        else None,
        compiler_params=pltpu.CompilerParams(vmem_limit_bytes=VMEM_LIMIT),
    )


def level(top):
    return jnp.ceil(STEPS * jnp.log2(jnp.maximum(top, 1e-30)))


def unit(steps):
    return jnp.exp2(steps * (1.0 / STEPS)) * (1.0 / TOP)


def to_code(x):
    return x.astype(jnp.int32).astype(jnp.int16)


def from_code(x):
    return x.astype(jnp.int32).astype(f32)


def panel_scales(spot, w_out, panel_ref, eo_ref, ei_ref):
    start = panel_ref[0, spot] * w_out
    row, shift = start // LANES, start % LANES
    last = eo_ref.shape[0] - 1
    spans = -(-w_out // LANES) + 1
    held = jnp.concatenate(
        [eo_ref[pl.ds(jnp.minimum(row + i, last), 1), :] for i in range(spans)], axis=1
    )
    picked = held[:, : w_out + PAD]
    for by in range(PAD, LANES, PAD):
        picked = jnp.where(shift == by, held[:, by : by + w_out + PAD], picked)
    e_in = ei_ref[pl.ds(panel_ref[1, spot], 1), :]
    return 1.0 / (picked + DAMPING), 1.0 / (e_in + DAMPING)


def split_body(bto_ref, bi_ref, out_ref):
    w_out, k_out = bto_ref.shape
    k_in = bi_ref.shape[0]
    rest = jnp.zeros((out_ref.shape[1] - w_out, k_out - k_in), bf16)
    for part, (b_out, b_in) in enumerate(zip(split2(bto_ref[...]), split2(bi_ref[...].T))):
        out_ref[part, :w_out, :] = b_out
        out_ref[part, w_out:, :k_in] = b_in
        out_ref[part, w_out:, k_in:] = rest


def rotate(rows, b_ref, w_out, k_out, k_in):
    n = rows.shape[0]
    w_pad = w_out + PAD
    lane = lax.broadcasted_iota(jnp.int32, (n, w_pad), 1)
    q_out, q_in = rows[:, :k_out], rows[:, k_out:]
    out = dot_nt(q_out, b_ref[0, :w_pad, :]) + dot_nt(q_out, b_ref[1, :w_pad, :])
    out = jnp.where(lane < w_out, out, 0.0)
    inn = dot_nt(q_in, b_ref[0, w_out:, :k_in]) + dot_nt(q_in, b_ref[1, w_out:, :k_in])
    s_out = level(jnp.max(jnp.abs(out), axis=1, keepdims=True))
    s_in = level(jnp.max(jnp.abs(inn), axis=1, keepdims=True))
    out = jnp.round(out * (1.0 / unit(s_out)))
    out = jnp.where(lane < w_out, out, jnp.where(lane < w_out + PAD // 2, s_out, s_in))
    inn = jnp.round(inn * (1.0 / unit(s_in)))
    return to_code(out), to_code(inn)


def rotate_own_body(
    n_out,
    n_in,
    w_out,
    at_ref,
    panel_ref,
    live_ref,
    eo_ref,
    ei_ref,
    q_ref,
    b_ref,
    rows_ref,
    code_ref,
    scale_ref,
    count_ref,
    wide,
):
    count_ref[...] = jnp.full(count_ref.shape, live_ref[0], jnp.int32)
    w_pad = w_out + PAD
    w_all = scale_ref.shape[1] // 2
    for k in range(2):
        s_out, s_in = panel_scales(at_ref[k], w_out, panel_ref, eo_ref, ei_ref)
        scale_ref[:, k * w_all : k * w_all + w_pad] = s_out
        scale_ref[:, k * w_all + w_pad : (k + 1) * w_all] = s_in
    n = q_ref.shape[0]
    wide[...] = q_ref[...].astype(f32).reshape(wide.shape)
    for r in range(n_out + n_in):
        rows_ref[:, r * LANES : (r + 1) * LANES] = wide[pl.ds(r, n, stride=SLOTS), :].astype(bf16)
    out, inn = rotate(rows_ref, b_ref, w_out, n_out * LANES, n_in * LANES)
    code_ref[:, : w_out + PAD] = out
    code_ref[:, w_out + PAD :] = inn


def rotate_mate_body(n_out, n_in, w_out, rows_ref, b_ref, code_ref, part_ref):
    out, inn = rotate(rows_ref, b_ref, w_out, n_out * LANES, n_in * LANES)
    w_all = code_ref.shape[1]
    for g in range(part_ref.shape[0]):
        part_ref[g, :, :w_all] = code_ref[...]
        part_ref[g, :, w_all : w_all + w_out + PAD] = out
        part_ref[g, :, w_all + w_out + PAD :] = inn


def restore_body(n_out, n_in, w_out, part_ref, scale_ref, own_ref, mate_ref, code_ref, wide):
    n = part_ref.shape[1]
    k_out, k_in = n_out * LANES, n_in * LANES
    w_in = own_ref.shape[1] - w_out
    w_pad = w_out + PAD
    w_all = w_pad + w_in
    lane = lax.broadcasted_iota(jnp.int32, (n, w_pad), 1)
    x_out = jnp.zeros((n, k_out), f32)
    x_in = jnp.zeros((n, k_in), f32)
    for k, b_ref in enumerate((own_ref, mate_ref)):
        at = k * w_all
        t_out = jnp.zeros((n, w_pad), f32)
        t_in = jnp.zeros((n, w_in), f32)
        for g in range(part_ref.shape[0]):
            x = from_code(part_ref[g, :, at : at + w_all])
            t_out += x[:, :w_pad] * unit(x[:, w_out : w_out + 1])
            t_in += x[:, w_pad:] * unit(x[:, w_out + PAD // 2 : w_out + PAD // 2 + 1])
        t_out = jnp.where(lane < w_out, t_out * scale_ref[:, at : at + w_pad], 0.0)
        t_in = t_in * scale_ref[:, at + w_pad : at + w_all]
        both = jnp.concatenate(split2(t_out), axis=0)
        x = dot_nn(both, b_ref[0, :w_pad, :])
        x_out += x[:n] + x[n:] + dot_nn(both[:n], b_ref[1, :w_pad, :])
        both = jnp.concatenate(split2(t_in), axis=0)
        x = dot_nn(both, b_ref[0, w_out:, :k_in])
        x_in += x[:n] + x[n:] + dot_nn(both[:n], b_ref[1, w_out:, :k_in])
    for first, x, row in ((0, x_out, n_out + n_in), (n_out, x_in, n_out + n_in + 1)):
        steps = level(jnp.max(jnp.abs(x), axis=1, keepdims=True))
        codes = jnp.round(x * (1.0 / unit(steps)))
        for r in range(x.shape[1] // LANES):
            wide[pl.ds(first + r, n, stride=SLOTS), :] = codes[:, r * LANES : (r + 1) * LANES]
        wide[pl.ds(row, n, stride=SLOTS), :] = jnp.broadcast_to(steps, (n, LANES))
    code_ref[...] = to_code(wide[...]).reshape(code_ref.shape)


def sum_codes_body(n_out, n_in, code_ref, out_ref):
    slot = lax.broadcasted_iota(jnp.int32, (SLOTS, LANES), 0)
    is_out = slot < n_out
    is_in = jnp.logical_and(slot >= n_out, slot < n_out + n_in)
    total = jnp.zeros((SLOTS, LANES), f32)
    for j in range(code_ref.shape[0]):
        x = from_code(code_ref[j])
        a = x[n_out + n_in : n_out + n_in + 1]
        b = x[n_out + n_in + 1 : n_out + n_in + 2]
        total = total + x * unit(jnp.where(is_out, a, b))
    size = jnp.abs(total)
    steps_out = level(jnp.max(jnp.where(is_out, size, 0.0), keepdims=True))
    steps_in = level(jnp.max(jnp.where(is_in, size, 0.0), keepdims=True))
    steps = jnp.where(is_out, steps_out, steps_in)
    codes = jnp.round(total * (1.0 / unit(steps)))
    codes = jnp.where(slot == n_out + n_in, steps_out, codes)
    codes = jnp.where(slot == n_out + n_in + 1, steps_in, codes)
    codes = to_code(codes)
    for j in range(out_ref.shape[0]):
        out_ref[j] = codes


def score_body(n_out, n_in, groups, count_ref, code_ref, to_ref, ti_ref, out_ref, wide, both):
    n = code_ref.shape[0] // groups
    rows = to_ref.shape[0]
    k_out = n_out * LANES
    along_out = jnp.zeros((2 * n, rows), f32)
    along_in = jnp.zeros((2 * n, rows), f32)
    for g in range(groups):
        x = from_code(code_ref[g * n : (g + 1) * n])
        wide[...] = x.reshape(wide.shape)
        for first, count, row in ((0, n_out, n_out + n_in), (n_out, n_in, n_out + n_in + 1)):
            scale = unit(wide[pl.ds(row, n, stride=SLOTS), :])
            for r in range(first, first + count):
                hi, lo = split2(wide[pl.ds(r, n, stride=SLOTS), :] * scale)
                both[:n, r * LANES : (r + 1) * LANES] = hi
                both[n:, r * LANES : (r + 1) * LANES] = lo
            width = count * LANES
            part = both[:, first * LANES : (first + count) * LANES]
            if first == 0:
                along_out += dot_nt(part, to_ref[:, g * width : (g + 1) * width])
            else:
                along_in += dot_nt(part, ti_ref[:, g * width : (g + 1) * width])
    product = (along_out[:n] + along_out[n:]) * (along_in[:n] + along_in[n:])
    span = 16 // NQ
    by_query = []
    for q in range(NQ):
        total = product[q * span : (q + 1) * span]
        for first in range((q + NQ) * span, n, NQ * span):
            total = total + product[first : first + span]
        by_query.append(jnp.sum(total, axis=0, keepdims=True))
    s_id = lax.broadcasted_iota(jnp.int32, (1, rows), 1) // RANK
    row = lax.broadcasted_iota(jnp.int32, out_ref.shape, 0)
    col = lax.broadcasted_iota(jnp.int32, out_ref.shape, 1)
    result = jnp.zeros(out_ref.shape, f32)
    for s in range(SEQ_DEV):
        for q in range(NQ):
            picked = jnp.where(s_id == s, by_query[q], 0.0)
            value = jnp.sum(picked, axis=1, keepdims=True) * (1.0 / RANK)
            result = jnp.where(jnp.logical_and(row == s, col == q), value, result)
    out_ref[...] = jnp.where(row < count_ref[:, :NQ], result, 0.0)


def spread(x, axes):
    n = lax.axis_size(axes)
    x = jnp.broadcast_to(x[None], (n, *x.shape))
    return lax.all_to_all(x, axes, split_axis=0, concat_axis=0, tiled=True)


def per_device(qo, qi, bo, bi, eo, ei, panels, to, ti, live):
    n_out, n_in = qo.shape[1] // LANES, qi.shape[1] // LANES
    data = n_out + n_in
    nz, nxl, nc = (lax.axis_size(a) for a in BLK)
    n_grp = lax.axis_size(GRP)
    half = nz * nxl
    n_rows = half * nc
    position = lax.axis_index(BLK)
    w_out, w_in = bo.shape[1], bi.shape[1]
    w_all = w_out + PAD + w_in

    own_q = jnp.concatenate([qo, qi], axis=1).reshape(data, LANES)
    own_q = jnp.pad(own_q, ((0, SLOTS - data), (0, 0)))
    queries = spread(own_q, ("z", "xl"))

    mate_spot = position + 1 - 2 * lax.axis_index("c")
    spots = jnp.stack([position, mate_spot]).astype(jnp.int32)
    own = call(
        split_body, jax.ShapeDtypeStruct((2, w_out + w_in, bo.shape[0]), bf16), n_in=2
    )(bo.T, bi)
    mate = lax.ppermute(own, "c", [(0, 1), (1, 0)])
    rows, own_part, scale, count = call(
        functools.partial(rotate_own_body, n_out, n_in, w_out),
        (
            jax.ShapeDtypeStruct((half, data * LANES), bf16),
            jax.ShapeDtypeStruct((half, w_all), jnp.int16),
            jax.ShapeDtypeStruct((1, nc * w_all), f32),
            jax.ShapeDtypeStruct((SEQ_DEV, LANES), jnp.int32),
        ),
        [pltpu.VMEM((half * SLOTS, LANES), f32)],
        n_in=7,
        smem=(0, 1, 2),
        flops=OWN_FLOPS,
    )(spots, panels, live, eo.reshape(-1, LANES), ei.reshape(-1, w_in), queries, own)
    part = call(
        functools.partial(rotate_mate_body, n_out, n_in, w_out),
        jax.ShapeDtypeStruct((n_grp, half, nc * w_all), jnp.int16),
        n_in=3,
    )(rows, mate, own_part)
    parts = lax.all_to_all(part, GRP, split_axis=0, concat_axis=0, tiled=True)

    codes = call(
        functools.partial(restore_body, n_out, n_in, w_out),
        jax.ShapeDtypeStruct((half, SLOTS, LANES), jnp.int16),
        [pltpu.VMEM((half * SLOTS, LANES), f32)],
        n_in=4,
    )(parts, scale, own, mate)
    codes = lax.all_to_all(codes, ("z", "xl"), split_axis=0, concat_axis=0, tiled=True)
    codes = call(
        functools.partial(sum_codes_body, n_out, n_in),
        jax.ShapeDtypeStruct((nz, SLOTS, LANES), jnp.int16),
    )(codes)
    codes = lax.all_to_all(codes, "z", split_axis=0, concat_axis=0, tiled=True)
    codes = lax.all_gather(codes, ("y", "xh", "xl", "c"), axis=0, tiled=True)
    return call(
        functools.partial(score_body, n_out, n_in, n_grp),
        jax.ShapeDtypeStruct((SEQ_DEV, NQ), f32),
        [
            pltpu.VMEM((n_rows * SLOTS, LANES), f32),
            pltpu.VMEM((2 * n_rows, data * LANES), bf16),
        ],
        n_in=4,
    )(count, codes, to, ti)


def solution(mesh):
    fine = Mesh(mesh.devices.reshape(4, 2, 16, 2, 2), GRP + BLK)
    in_specs = (
        P(BLK, GRP),
        P(BLK, GRP),
        P(GRP, BLK),
        P(GRP, BLK),
        P(),
        P(),
        P(),
        P(GRP + BLK, None),
        P(GRP + BLK, None),
        P(GRP + BLK),
    )
    out_specs = P(GRP + BLK, None)
    return jax.shard_map(
        per_device, mesh=fine, in_specs=in_specs, out_specs=out_specs, check_vma=False
    )
```

```python
import functools

import jax
import jax.numpy as jnp
from jax import lax
from jax.experimental import pallas as pl
from jax.experimental.pallas import tpu as pltpu
from jax.sharding import Mesh
from jax.sharding import PartitionSpec as P

NQ = 2
SEQ_DEV = 2
RANK = 32
DAMPING = 0.5
LANES = 128
SLOTS = 24
STEPS = 8
TOP = 32766.0
OWN_FLOPS = 20_000_000_000
PAD = 32
GRP = ("y", "xh")
BLK = ("z", "xl", "c")
VMEM_LIMIT = 12 * 1024 * 1024

f32 = jnp.float32
bf16 = jnp.bfloat16


def split2(x):
    hi = x.astype(bf16)
    return hi, (x - hi.astype(f32)).astype(bf16)


def dot_nn(a, b):
    return lax.dot_general(a, b, (((1,), (0,)), ((), ())), preferred_element_type=f32)


def dot_nt(a, b):
    return lax.dot_general(a, b, (((1,), (1,)), ((), ())), preferred_element_type=f32)


def call(body, out_shape, scratch=(), n_in=1, smem=(), flops=0):
    specs = [
        pl.BlockSpec(memory_space=pltpu.SMEM if i in smem else pltpu.VMEM) for i in range(n_in)
    ]
    outs = jax.tree.map(lambda _: pl.BlockSpec(memory_space=pltpu.VMEM), out_shape)
    return pl.pallas_call(
        body,
        out_shape=out_shape,
        in_specs=specs,
        out_specs=outs,
        scratch_shapes=list(scratch),
        cost_estimate=pl.CostEstimate(flops=flops, bytes_accessed=0, transcendentals=0)
        if flops
        else None,
        compiler_params=pltpu.CompilerParams(vmem_limit_bytes=VMEM_LIMIT),
    )


def level(top):
    return jnp.ceil(STEPS * jnp.log2(jnp.maximum(top, 1e-30)))


def unit(steps):
    return jnp.exp2(steps * (1.0 / STEPS)) * (1.0 / TOP)


def to_code(x):
    return x.astype(jnp.int32).astype(jnp.int16)


def from_code(x):
    return x.astype(jnp.int32).astype(f32)


def panel_scales(spot, w_out, panel_ref, eo_ref, ei_ref):
    start = panel_ref[0, spot] * w_out
    row, shift = start // LANES, start % LANES
    last = eo_ref.shape[0] - 1
    spans = -(-w_out // LANES) + 1
    held = jnp.concatenate(
        [eo_ref[pl.ds(jnp.minimum(row + i, last), 1), :] for i in range(spans)], axis=1
    )
    picked = held[:, : w_out + PAD]
    for by in range(PAD, LANES, PAD):
        picked = jnp.where(shift == by, held[:, by : by + w_out + PAD], picked)
    e_in = ei_ref[pl.ds(panel_ref[1, spot], 1), :]
    return 1.0 / (picked + DAMPING), 1.0 / (e_in + DAMPING)


def split_body(bto_ref, bi_ref, out_ref):
    w_out, k_out = bto_ref.shape
    k_in = bi_ref.shape[0]
    rest = jnp.zeros((out_ref.shape[1] - w_out, k_out - k_in), bf16)
    for part, (b_out, b_in) in enumerate(zip(split2(bto_ref[...]), split2(bi_ref[...].T))):
        out_ref[part, :w_out, :] = b_out
        out_ref[part, w_out:, :k_in] = b_in
        out_ref[part, w_out:, k_in:] = rest


def rotate(rows, b_ref, w_out, k_out, k_in):
    n = rows.shape[0]
    w_pad = w_out + PAD
    lane = lax.broadcasted_iota(jnp.int32, (n, w_pad), 1)
    q_out, q_in = rows[:, :k_out], rows[:, k_out:]
    out = dot_nt(q_out, b_ref[0, :w_pad, :]) + dot_nt(q_out, b_ref[1, :w_pad, :])
    out = jnp.where(lane < w_out, out, 0.0)
    inn = dot_nt(q_in, b_ref[0, w_out:, :k_in]) + dot_nt(q_in, b_ref[1, w_out:, :k_in])
    s_out = level(jnp.max(jnp.abs(out), axis=1, keepdims=True))
    s_in = level(jnp.max(jnp.abs(inn), axis=1, keepdims=True))
    out = jnp.round(out * (1.0 / unit(s_out)))
    out = jnp.where(lane < w_out, out, jnp.where(lane < w_out + PAD // 2, s_out, s_in))
    inn = jnp.round(inn * (1.0 / unit(s_in)))
    return to_code(out), to_code(inn)


def rotate_own_body(
    n_out,
    n_in,
    w_out,
    at_ref,
    panel_ref,
    live_ref,
    eo_ref,
    ei_ref,
    q_ref,
    b_ref,
    rows_ref,
    code_ref,
    scale_ref,
    count_ref,
    wide,
):
    count_ref[...] = jnp.full(count_ref.shape, live_ref[0], jnp.int32)
    w_pad = w_out + PAD
    w_all = scale_ref.shape[1] // 2
    for k in range(2):
        s_out, s_in = panel_scales(at_ref[k], w_out, panel_ref, eo_ref, ei_ref)
        scale_ref[:, k * w_all : k * w_all + w_pad] = s_out
        scale_ref[:, k * w_all + w_pad : (k + 1) * w_all] = s_in
    n = q_ref.shape[0]
    wide[...] = q_ref[...].astype(f32).reshape(wide.shape)
    for r in range(n_out + n_in):
        rows_ref[:, r * LANES : (r + 1) * LANES] = wide[pl.ds(r, n, stride=SLOTS), :].astype(bf16)
    out, inn = rotate(rows_ref, b_ref, w_out, n_out * LANES, n_in * LANES)
    code_ref[:, : w_out + PAD] = out
    code_ref[:, w_out + PAD :] = inn


def rotate_mate_body(n_out, n_in, w_out, rows_ref, b_ref, code_ref, part_ref):
    out, inn = rotate(rows_ref, b_ref, w_out, n_out * LANES, n_in * LANES)
    w_all = code_ref.shape[1]
    for g in range(part_ref.shape[0]):
        part_ref[g, :, :w_all] = code_ref[...]
        part_ref[g, :, w_all : w_all + w_out + PAD] = out
        part_ref[g, :, w_all + w_out + PAD :] = inn


def restore_body(n_out, n_in, w_out, part_ref, scale_ref, own_ref, mate_ref, code_ref, wide):
    n = part_ref.shape[1]
    k_out, k_in = n_out * LANES, n_in * LANES
    w_in = own_ref.shape[1] - w_out
    w_pad = w_out + PAD
    w_all = w_pad + w_in
    lane = lax.broadcasted_iota(jnp.int32, (n, w_pad), 1)
    x_out = jnp.zeros((n, k_out), f32)
    x_in = jnp.zeros((n, k_in), f32)
    for k, b_ref in enumerate((own_ref, mate_ref)):
        at = k * w_all
        t_out = jnp.zeros((n, w_pad), f32)
        t_in = jnp.zeros((n, w_in), f32)
        for g in range(part_ref.shape[0]):
            x = from_code(part_ref[g, :, at : at + w_all])
            t_out += x[:, :w_pad] * unit(x[:, w_out : w_out + 1])
            t_in += x[:, w_pad:] * unit(x[:, w_out + PAD // 2 : w_out + PAD // 2 + 1])
        t_out = jnp.where(lane < w_out, t_out * scale_ref[:, at : at + w_pad], 0.0)
        t_in = t_in * scale_ref[:, at + w_pad : at + w_all]
        both = jnp.concatenate(split2(t_out), axis=0)
        x = dot_nn(both, b_ref[0, :w_pad, :])
        x_out += x[:n] + x[n:] + dot_nn(both[:n], b_ref[1, :w_pad, :])
        both = jnp.concatenate(split2(t_in), axis=0)
        x = dot_nn(both, b_ref[0, w_out:, :k_in])
        x_in += x[:n] + x[n:] + dot_nn(both[:n], b_ref[1, w_out:, :k_in])
    for first, x, row in ((0, x_out, n_out + n_in), (n_out, x_in, n_out + n_in + 1)):
        steps = level(jnp.max(jnp.abs(x), axis=1, keepdims=True))
        codes = jnp.round(x * (1.0 / unit(steps)))
        for r in range(x.shape[1] // LANES):
            wide[pl.ds(first + r, n, stride=SLOTS), :] = codes[:, r * LANES : (r + 1) * LANES]
        wide[pl.ds(row, n, stride=SLOTS), :] = jnp.broadcast_to(steps, (n, LANES))
    code_ref[...] = to_code(wide[...]).reshape(code_ref.shape)


def sum_codes_body(n_out, n_in, code_ref, out_ref):
    slot = lax.broadcasted_iota(jnp.int32, (SLOTS, LANES), 0)
    is_out = slot < n_out
    is_in = jnp.logical_and(slot >= n_out, slot < n_out + n_in)
    total = jnp.zeros((SLOTS, LANES), f32)
    for j in range(code_ref.shape[0]):
        x = from_code(code_ref[j])
        a = x[n_out + n_in : n_out + n_in + 1]
        b = x[n_out + n_in + 1 : n_out + n_in + 2]
        total = total + x * unit(jnp.where(is_out, a, b))
    size = jnp.abs(total)
    steps_out = level(jnp.max(jnp.where(is_out, size, 0.0), keepdims=True))
    steps_in = level(jnp.max(jnp.where(is_in, size, 0.0), keepdims=True))
    steps = jnp.where(is_out, steps_out, steps_in)
    codes = jnp.round(total * (1.0 / unit(steps)))
    codes = jnp.where(slot == n_out + n_in, steps_out, codes)
    codes = jnp.where(slot == n_out + n_in + 1, steps_in, codes)
    codes = to_code(codes)
    for j in range(out_ref.shape[0]):
        out_ref[j] = codes


def score_body(n_out, n_in, groups, count_ref, code_ref, to_ref, ti_ref, out_ref, wide):
    n = code_ref.shape[0] // groups
    rows = to_ref.shape[0]
    alongs = [jnp.zeros((2 * n, rows), f32)] * 2
    sides = ((0, n_out, to_ref), (n_out, n_in, ti_ref))
    for g in range(groups):
        wide[...] = from_code(code_ref[g * n : (g + 1) * n]).reshape(wide.shape)

        def row(r):
            return wide[pl.ds(r, n, stride=SLOTS), :]

        for side, (first, count, t_ref) in enumerate(sides):
            scale = unit(row(n_out + n_in + side))
            scale = jnp.concatenate([scale, scale], axis=1)
            for r in range(0, count, 2):
                pair = jnp.concatenate([row(first + r), row(first + r + 1)], axis=1)
                both = jnp.concatenate(split2(pair * scale), axis=0)
                at = (g * count + r) * LANES
                alongs[side] += dot_nt(both, t_ref[:, at : at + 2 * LANES])
    along_out, along_in = alongs
    product = (along_out[:n] + along_out[n:]) * (along_in[:n] + along_in[n:])
    span = 16 // NQ
    by_query = []
    for q in range(NQ):
        total = product[q * span : (q + 1) * span]
        for first in range((q + NQ) * span, n, NQ * span):
            total = total + product[first : first + span]
        by_query.append(jnp.sum(total, axis=0, keepdims=True))
    s_id = lax.broadcasted_iota(jnp.int32, (1, rows), 1) // RANK
    row = lax.broadcasted_iota(jnp.int32, out_ref.shape, 0)
    col = lax.broadcasted_iota(jnp.int32, out_ref.shape, 1)
    result = jnp.zeros(out_ref.shape, f32)
    for s in range(SEQ_DEV):
        for q in range(NQ):
            picked = jnp.where(s_id == s, by_query[q], 0.0)
            value = jnp.sum(picked, axis=1, keepdims=True) * (1.0 / RANK)
            result = jnp.where(jnp.logical_and(row == s, col == q), value, result)
    out_ref[...] = jnp.where(row < count_ref[:, :NQ], result, 0.0)


def spread(x, axes):
    n = lax.axis_size(axes)
    x = jnp.broadcast_to(x[None], (n, *x.shape))
    return lax.all_to_all(x, axes, split_axis=0, concat_axis=0, tiled=True)


def per_device(qo, qi, bo, bi, eo, ei, panels, to, ti, live):
    n_out, n_in = qo.shape[1] // LANES, qi.shape[1] // LANES
    data = n_out + n_in
    nz, nxl, nc = (lax.axis_size(a) for a in BLK)
    n_grp = lax.axis_size(GRP)
    half = nz * nxl
    n_rows = half * nc
    position = lax.axis_index(BLK)
    w_out, w_in = bo.shape[1], bi.shape[1]
    w_all = w_out + PAD + w_in

    own_q = jnp.concatenate([qo, qi], axis=1).reshape(data, LANES)
    own_q = jnp.pad(own_q, ((0, SLOTS - data), (0, 0)))
    queries = spread(own_q, ("z", "xl"))

    mate_spot = position + 1 - 2 * lax.axis_index("c")
    spots = jnp.stack([position, mate_spot]).astype(jnp.int32)
    own = call(
        split_body, jax.ShapeDtypeStruct((2, w_out + w_in, bo.shape[0]), bf16), n_in=2
    )(bo.T, bi)
    mate = lax.ppermute(own, "c", [(0, 1), (1, 0)])
    rows, own_part, scale, count = call(
        functools.partial(rotate_own_body, n_out, n_in, w_out),
        (
            jax.ShapeDtypeStruct((half, data * LANES), bf16),
            jax.ShapeDtypeStruct((half, w_all), jnp.int16),
            jax.ShapeDtypeStruct((1, nc * w_all), f32),
            jax.ShapeDtypeStruct((SEQ_DEV, LANES), jnp.int32),
        ),
        [pltpu.VMEM((half * SLOTS, LANES), f32)],
        n_in=7,
        smem=(0, 1, 2),
        flops=OWN_FLOPS,
    )(spots, panels, live, eo.reshape(-1, LANES), ei.reshape(-1, w_in), queries, own)
    part = call(
        functools.partial(rotate_mate_body, n_out, n_in, w_out),
        jax.ShapeDtypeStruct((n_grp, half, nc * w_all), jnp.int16),
        n_in=3,
    )(rows, mate, own_part)
    parts = lax.all_to_all(part, GRP, split_axis=0, concat_axis=0, tiled=True)

    codes = call(
        functools.partial(restore_body, n_out, n_in, w_out),
        jax.ShapeDtypeStruct((half, SLOTS, LANES), jnp.int16),
        [pltpu.VMEM((half * SLOTS, LANES), f32)],
        n_in=4,
    )(parts, scale, own, mate)
    codes = lax.all_to_all(codes, ("z", "xl"), split_axis=0, concat_axis=0, tiled=True)
    codes = call(
        functools.partial(sum_codes_body, n_out, n_in),
        jax.ShapeDtypeStruct((nz, SLOTS, LANES), jnp.int16),
    )(codes)
    codes = lax.all_to_all(codes, "z", split_axis=0, concat_axis=0, tiled=True)
    codes = lax.all_gather(codes, ("y", "xh", "xl", "c"), axis=0, tiled=True)
    return call(
        functools.partial(score_body, n_out, n_in, n_grp),
        jax.ShapeDtypeStruct((SEQ_DEV, NQ), f32),
        [
            pltpu.VMEM((n_rows * SLOTS, LANES), f32),
        ],
        n_in=4,
    )(count, codes, to, ti)


def solution(mesh):
    fine = Mesh(mesh.devices.reshape(4, 2, 16, 2, 2), GRP + BLK)
    in_specs = (
        P(BLK, GRP),
        P(BLK, GRP),
        P(GRP, BLK),
        P(GRP, BLK),
        P(),
        P(),
        P(),
        P(GRP + BLK, None),
        P(GRP + BLK, None),
        P(GRP + BLK),
    )
    out_specs = P(GRP + BLK, None)
    return jax.shard_map(
        per_device, mesh=fine, in_specs=in_specs, out_specs=out_specs, check_vma=False
    )
```

```python
import functools

import jax
import jax.numpy as jnp
from jax import lax
from jax.experimental import pallas as pl
from jax.experimental.pallas import tpu as pltpu
from jax.sharding import Mesh
from jax.sharding import PartitionSpec as P

NQ = 2
SEQ_DEV = 2
RANK = 32
DAMPING = 0.5
LANES = 128
SLOTS = 24
STEPS = 8
TOP = 32766.0
OWN_FLOPS = 20_000_000_000
PAD = 32
GRP = ("y", "xh")
BLK = ("z", "xl", "c")
VMEM_LIMIT = 12 * 1024 * 1024

f32 = jnp.float32
bf16 = jnp.bfloat16


def split2(x):
    hi = x.astype(bf16)
    return hi, (x - hi.astype(f32)).astype(bf16)


def dot_nn(a, b):
    return lax.dot_general(a, b, (((1,), (0,)), ((), ())), preferred_element_type=f32)


def dot_nt(a, b):
    return lax.dot_general(a, b, (((1,), (1,)), ((), ())), preferred_element_type=f32)


def call(body, out_shape, scratch=(), n_in=1, smem=(), flops=0):
    specs = [
        pl.BlockSpec(memory_space=pltpu.SMEM if i in smem else pltpu.VMEM) for i in range(n_in)
    ]
    outs = jax.tree.map(lambda _: pl.BlockSpec(memory_space=pltpu.VMEM), out_shape)
    return pl.pallas_call(
        body,
        out_shape=out_shape,
        in_specs=specs,
        out_specs=outs,
        scratch_shapes=list(scratch),
        cost_estimate=pl.CostEstimate(flops=flops, bytes_accessed=0, transcendentals=0)
        if flops
        else None,
        compiler_params=pltpu.CompilerParams(vmem_limit_bytes=VMEM_LIMIT),
    )


def level(top):
    return jnp.ceil(STEPS * jnp.log2(jnp.maximum(top, 1e-30)))


def unit(steps):
    return jnp.exp2(steps * (1.0 / STEPS)) * (1.0 / TOP)


def to_code(x):
    return x.astype(jnp.int32).astype(jnp.int16)


def from_code(x):
    return x.astype(jnp.int32).astype(f32)


def panel_scales(spot, w_out, panel_ref, eo_ref, ei_ref):
    start = panel_ref[0, spot] * w_out
    row, shift = start // LANES, start % LANES
    last = eo_ref.shape[0] - 1
    spans = -(-w_out // LANES) + 1
    held = jnp.concatenate(
        [eo_ref[pl.ds(jnp.minimum(row + i, last), 1), :] for i in range(spans)], axis=1
    )
    picked = held[:, : w_out + PAD]
    for by in range(PAD, LANES, PAD):
        picked = jnp.where(shift == by, held[:, by : by + w_out + PAD], picked)
    e_in = ei_ref[pl.ds(panel_ref[1, spot], 1), :]
    return 1.0 / (picked + DAMPING), 1.0 / (e_in + DAMPING)


def split_body(bto_ref, bi_ref, out_ref):
    w_out, k_out = bto_ref.shape
    k_in = bi_ref.shape[0]
    rest = jnp.zeros((out_ref.shape[1] - w_out, k_out - k_in), bf16)
    for part, (b_out, b_in) in enumerate(zip(split2(bto_ref[...]), split2(bi_ref[...].T))):
        out_ref[part, :w_out, :] = b_out
        out_ref[part, w_out:, :k_in] = b_in
        out_ref[part, w_out:, k_in:] = rest


def rotate(rows, b_ref, w_out, k_out, k_in):
    n = rows.shape[0]
    w_pad = w_out + PAD
    lane = lax.broadcasted_iota(jnp.int32, (n, w_pad), 1)
    q_out, q_in = rows[:, :k_out], rows[:, k_out:]
    out = dot_nt(q_out, b_ref[0, :w_pad, :]) + dot_nt(q_out, b_ref[1, :w_pad, :])
    out = jnp.where(lane < w_out, out, 0.0)
    inn = dot_nt(q_in, b_ref[0, w_out:, :k_in]) + dot_nt(q_in, b_ref[1, w_out:, :k_in])
    s_out = level(jnp.max(jnp.abs(out), axis=1, keepdims=True))
    s_in = level(jnp.max(jnp.abs(inn), axis=1, keepdims=True))
    out = jnp.round(out * (1.0 / unit(s_out)))
    out = jnp.where(lane < w_out, out, jnp.where(lane < w_out + PAD // 2, s_out, s_in))
    inn = jnp.round(inn * (1.0 / unit(s_in)))
    return to_code(out), to_code(inn)


def rotate_own_body(
    n_out,
    n_in,
    w_out,
    at_ref,
    panel_ref,
    live_ref,
    eo_ref,
    ei_ref,
    q_ref,
    b_ref,
    rows_ref,
    code_ref,
    scale_ref,
    count_ref,
    wide,
):
    count_ref[...] = jnp.full(count_ref.shape, live_ref[0], jnp.int32)
    w_pad = w_out + PAD
    w_all = scale_ref.shape[1] // 2
    for k in range(2):
        s_out, s_in = panel_scales(at_ref[k], w_out, panel_ref, eo_ref, ei_ref)
        scale_ref[:, k * w_all : k * w_all + w_pad] = s_out
        scale_ref[:, k * w_all + w_pad : (k + 1) * w_all] = s_in
    n = q_ref.shape[0]
    wide[...] = q_ref[...].astype(f32).reshape(wide.shape)
    for r in range(n_out + n_in):
        rows_ref[:, r * LANES : (r + 1) * LANES] = wide[pl.ds(r, n, stride=SLOTS), :].astype(bf16)
    out, inn = rotate(rows_ref, b_ref, w_out, n_out * LANES, n_in * LANES)
    code_ref[:, : w_out + PAD] = out
    code_ref[:, w_out + PAD :] = inn


def rotate_mate_body(n_out, n_in, w_out, rows_ref, b_ref, code_ref, part_ref):
    out, inn = rotate(rows_ref, b_ref, w_out, n_out * LANES, n_in * LANES)
    w_all = code_ref.shape[1]
    for g in range(part_ref.shape[0]):
        part_ref[g, :, :w_all] = code_ref[...]
        part_ref[g, :, w_all : w_all + w_out + PAD] = out
        part_ref[g, :, w_all + w_out + PAD :] = inn


def back(both, b_hi, b_lo):
    n = both.shape[0] // 2
    x = dot_nn(both, b_hi)
    return x[:n] + x[n:] + dot_nn(both[:n], b_lo)


def restore_own_body(
    n_out, n_in, w_out, part_ref, scale_ref, own_ref, x_ref, mate_out_ref, mate_in_ref
):
    n = part_ref.shape[1]
    k_out, k_in = n_out * LANES, n_in * LANES
    w_in = own_ref.shape[1] - w_out
    w_pad = w_out + PAD
    w_all = w_pad + w_in
    lane = lax.broadcasted_iota(jnp.int32, (n, w_pad), 1)
    for k in range(2):
        at = k * w_all
        t_out = jnp.zeros((n, w_pad), f32)
        t_in = jnp.zeros((n, w_in), f32)
        for g in range(part_ref.shape[0]):
            x = from_code(part_ref[g, :, at : at + w_all])
            t_out += x[:, :w_pad] * unit(x[:, w_out : w_out + 1])
            t_in += x[:, w_pad:] * unit(x[:, w_out + PAD // 2 : w_out + PAD // 2 + 1])
        t_out = jnp.where(lane < w_out, t_out * scale_ref[:, at : at + w_pad], 0.0)
        t_in = t_in * scale_ref[:, at + w_pad : at + w_all]
        t_out = jnp.concatenate(split2(t_out), axis=0)
        t_in = jnp.concatenate(split2(t_in), axis=0)
        if k == 0:
            x_ref[:, :k_out] = back(t_out, own_ref[0, :w_pad, :], own_ref[1, :w_pad, :])
            x_ref[:, k_out:] = back(t_in, own_ref[0, w_out:, :k_in], own_ref[1, w_out:, :k_in])
        else:
            mate_out_ref[...] = t_out
            mate_in_ref[...] = t_in


def restore_mate_body(
    n_out, n_in, w_out, x_ref, mate_out_ref, mate_in_ref, mate_ref, code_ref, wide
):
    n = x_ref.shape[0]
    k_out, k_in = n_out * LANES, n_in * LANES
    w_pad = w_out + PAD
    x_out = x_ref[:, :k_out] + back(
        mate_out_ref[...], mate_ref[0, :w_pad, :], mate_ref[1, :w_pad, :]
    )
    x_in = x_ref[:, k_out:] + back(
        mate_in_ref[...], mate_ref[0, w_out:, :k_in], mate_ref[1, w_out:, :k_in]
    )
    for first, x, row in ((0, x_out, n_out + n_in), (n_out, x_in, n_out + n_in + 1)):
        steps = level(jnp.max(jnp.abs(x), axis=1, keepdims=True))
        codes = jnp.round(x * (1.0 / unit(steps)))
        for r in range(x.shape[1] // LANES):
            wide[pl.ds(first + r, n, stride=SLOTS), :] = codes[:, r * LANES : (r + 1) * LANES]
        wide[pl.ds(row, n, stride=SLOTS), :] = jnp.broadcast_to(steps, (n, LANES))
    code_ref[...] = to_code(wide[...]).reshape(code_ref.shape)


def sum_codes_body(n_out, n_in, code_ref, out_ref):
    slot = lax.broadcasted_iota(jnp.int32, (SLOTS, LANES), 0)
    is_out = slot < n_out
    is_in = jnp.logical_and(slot >= n_out, slot < n_out + n_in)
    total = jnp.zeros((SLOTS, LANES), f32)
    for j in range(code_ref.shape[0]):
        x = from_code(code_ref[j])
        a = x[n_out + n_in : n_out + n_in + 1]
        b = x[n_out + n_in + 1 : n_out + n_in + 2]
        total = total + x * unit(jnp.where(is_out, a, b))
    size = jnp.abs(total)
    steps_out = level(jnp.max(jnp.where(is_out, size, 0.0), keepdims=True))
    steps_in = level(jnp.max(jnp.where(is_in, size, 0.0), keepdims=True))
    steps = jnp.where(is_out, steps_out, steps_in)
    codes = jnp.round(total * (1.0 / unit(steps)))
    codes = jnp.where(slot == n_out + n_in, steps_out, codes)
    codes = jnp.where(slot == n_out + n_in + 1, steps_in, codes)
    codes = to_code(codes)
    for j in range(out_ref.shape[0]):
        out_ref[j] = codes


def score_body(n_out, n_in, groups, count_ref, code_ref, to_ref, ti_ref, out_ref, wide):
    n = code_ref.shape[0] // groups
    rows = to_ref.shape[0]
    alongs = [jnp.zeros((2 * n, rows), f32)] * 2
    sides = ((0, n_out, to_ref), (n_out, n_in, ti_ref))
    for g in range(groups):
        wide[...] = from_code(code_ref[g * n : (g + 1) * n]).reshape(wide.shape)

        def row(r):
            return wide[pl.ds(r, n, stride=SLOTS), :]

        for side, (first, count, t_ref) in enumerate(sides):
            scale = unit(row(n_out + n_in + side))
            scale = jnp.concatenate([scale, scale], axis=1)
            for r in range(0, count, 2):
                pair = jnp.concatenate([row(first + r), row(first + r + 1)], axis=1)
                both = jnp.concatenate(split2(pair * scale), axis=0)
                at = (g * count + r) * LANES
                alongs[side] += dot_nt(both, t_ref[:, at : at + 2 * LANES])
    along_out, along_in = alongs
    product = (along_out[:n] + along_out[n:]) * (along_in[:n] + along_in[n:])
    span = 16 // NQ
    by_query = []
    for q in range(NQ):
        total = product[q * span : (q + 1) * span]
        for first in range((q + NQ) * span, n, NQ * span):
            total = total + product[first : first + span]
        by_query.append(jnp.sum(total, axis=0, keepdims=True))
    s_id = lax.broadcasted_iota(jnp.int32, (1, rows), 1) // RANK
    row = lax.broadcasted_iota(jnp.int32, out_ref.shape, 0)
    col = lax.broadcasted_iota(jnp.int32, out_ref.shape, 1)
    result = jnp.zeros(out_ref.shape, f32)
    for s in range(SEQ_DEV):
        for q in range(NQ):
            picked = jnp.where(s_id == s, by_query[q], 0.0)
            value = jnp.sum(picked, axis=1, keepdims=True) * (1.0 / RANK)
            result = jnp.where(jnp.logical_and(row == s, col == q), value, result)
    out_ref[...] = jnp.where(row < count_ref[:, :NQ], result, 0.0)


def spread(x, axes):
    n = lax.axis_size(axes)
    x = jnp.broadcast_to(x[None], (n, *x.shape))
    return lax.all_to_all(x, axes, split_axis=0, concat_axis=0, tiled=True)


def per_device(qo, qi, bo, bi, eo, ei, panels, to, ti, live):
    n_out, n_in = qo.shape[1] // LANES, qi.shape[1] // LANES
    data = n_out + n_in
    nz, nxl, nc = (lax.axis_size(a) for a in BLK)
    n_grp = lax.axis_size(GRP)
    half = nz * nxl
    n_rows = half * nc
    position = lax.axis_index(BLK)
    w_out, w_in = bo.shape[1], bi.shape[1]
    w_all = w_out + PAD + w_in

    own_q = jnp.concatenate([qo, qi], axis=1).reshape(data, LANES)
    own_q = jnp.pad(own_q, ((0, SLOTS - data), (0, 0)))
    queries = spread(own_q, ("z", "xl"))

    mate_spot = position + 1 - 2 * lax.axis_index("c")
    spots = jnp.stack([position, mate_spot]).astype(jnp.int32)
    own = call(
        split_body, jax.ShapeDtypeStruct((2, w_out + w_in, bo.shape[0]), bf16), n_in=2
    )(bo.T, bi)
    mate = lax.ppermute(own, "c", [(0, 1), (1, 0)])
    rows, own_part, scale, count = call(
        functools.partial(rotate_own_body, n_out, n_in, w_out),
        (
            jax.ShapeDtypeStruct((half, data * LANES), bf16),
            jax.ShapeDtypeStruct((half, w_all), jnp.int16),
            jax.ShapeDtypeStruct((1, nc * w_all), f32),
            jax.ShapeDtypeStruct((SEQ_DEV, LANES), jnp.int32),
        ),
        [pltpu.VMEM((half * SLOTS, LANES), f32)],
        n_in=7,
        smem=(0, 1, 2),
        flops=OWN_FLOPS,
    )(spots, panels, live, eo.reshape(-1, LANES), ei.reshape(-1, w_in), queries, own)
    part = call(
        functools.partial(rotate_mate_body, n_out, n_in, w_out),
        jax.ShapeDtypeStruct((n_grp, half, nc * w_all), jnp.int16),
        n_in=3,
    )(rows, mate, own_part)
    parts = lax.all_to_all(part, GRP, split_axis=0, concat_axis=0, tiled=True)

    x_own, mate_out, mate_in = call(
        functools.partial(restore_own_body, n_out, n_in, w_out),
        (
            jax.ShapeDtypeStruct((half, data * LANES), f32),
            jax.ShapeDtypeStruct((2 * half, w_out + PAD), bf16),
            jax.ShapeDtypeStruct((2 * half, w_in), bf16),
        ),
        n_in=3,
        flops=OWN_FLOPS,
    )(parts, scale, own)
    codes = call(
        functools.partial(restore_mate_body, n_out, n_in, w_out),
        jax.ShapeDtypeStruct((half, SLOTS, LANES), jnp.int16),
        [pltpu.VMEM((half * SLOTS, LANES), f32)],
        n_in=4,
    )(x_own, mate_out, mate_in, mate)
    codes = lax.all_to_all(codes, ("z", "xl"), split_axis=0, concat_axis=0, tiled=True)
    codes = call(
        functools.partial(sum_codes_body, n_out, n_in),
        jax.ShapeDtypeStruct((nz, SLOTS, LANES), jnp.int16),
    )(codes)
    codes = lax.all_to_all(codes, "z", split_axis=0, concat_axis=0, tiled=True)
    codes = lax.all_gather(codes, ("y", "xh", "xl", "c"), axis=0, tiled=True)
    return call(
        functools.partial(score_body, n_out, n_in, n_grp),
        jax.ShapeDtypeStruct((SEQ_DEV, NQ), f32),
        [
            pltpu.VMEM((n_rows * SLOTS, LANES), f32),
        ],
        n_in=4,
    )(count, codes, to, ti)


def solution(mesh):
    fine = Mesh(mesh.devices.reshape(4, 2, 16, 2, 2), GRP + BLK)
    in_specs = (
        P(BLK, GRP),
        P(BLK, GRP),
        P(GRP, BLK),
        P(GRP, BLK),
        P(),
        P(),
        P(),
        P(GRP + BLK, None),
        P(GRP + BLK, None),
        P(GRP + BLK),
    )
    out_specs = P(GRP + BLK, None)
    return jax.shard_map(
        per_device, mesh=fine, in_specs=in_specs, out_specs=out_specs, check_vma=False
    )
```

```python
import functools

import jax
import jax.numpy as jnp
from jax import lax
from jax.experimental import pallas as pl
from jax.experimental.pallas import tpu as pltpu
from jax.sharding import Mesh
from jax.sharding import PartitionSpec as P

NQ = 2
SEQ_DEV = 2
RANK = 32
DAMPING = 0.5
LANES = 128
SLOTS = 24
STEPS = 8
TOP = 32766.0
OWN_FLOPS = 20_000_000_000
PAD = 32
GRP = ("y", "xh")
BLK = ("z", "xl", "c")
VMEM_LIMIT = 12 * 1024 * 1024

f32 = jnp.float32
bf16 = jnp.bfloat16


def split2(x):
    hi = x.astype(bf16)
    return hi, (x - hi.astype(f32)).astype(bf16)


def dot_nn(a, b):
    return lax.dot_general(a, b, (((1,), (0,)), ((), ())), preferred_element_type=f32)


def dot_nt(a, b):
    return lax.dot_general(a, b, (((1,), (1,)), ((), ())), preferred_element_type=f32)


def call(body, out_shape, scratch=(), n_in=1, smem=(), flops=0):
    specs = [
        pl.BlockSpec(memory_space=pltpu.SMEM if i in smem else pltpu.VMEM) for i in range(n_in)
    ]
    outs = jax.tree.map(lambda _: pl.BlockSpec(memory_space=pltpu.VMEM), out_shape)
    return pl.pallas_call(
        body,
        out_shape=out_shape,
        in_specs=specs,
        out_specs=outs,
        scratch_shapes=list(scratch),
        cost_estimate=pl.CostEstimate(flops=flops, bytes_accessed=0, transcendentals=0)
        if flops
        else None,
        compiler_params=pltpu.CompilerParams(vmem_limit_bytes=VMEM_LIMIT),
    )


def level(top):
    return jnp.ceil(STEPS * jnp.log2(jnp.maximum(top, 1e-30)))


def unit(steps):
    return jnp.exp2(steps * (1.0 / STEPS)) * (1.0 / TOP)


def to_code(x):
    return x.astype(jnp.int32).astype(jnp.int16)


def from_code(x):
    return x.astype(jnp.int32).astype(f32)


def panel_scales(spot, w_out, panel_ref, eo_ref, ei_ref):
    start = panel_ref[0, spot] * w_out
    row, shift = start // LANES, start % LANES
    last = eo_ref.shape[0] - 1
    spans = -(-w_out // LANES) + 1
    held = jnp.concatenate(
        [eo_ref[pl.ds(jnp.minimum(row + i, last), 1), :] for i in range(spans)], axis=1
    )
    picked = held[:, : w_out + PAD]
    for by in range(PAD, LANES, PAD):
        picked = jnp.where(shift == by, held[:, by : by + w_out + PAD], picked)
    e_in = ei_ref[pl.ds(panel_ref[1, spot], 1), :]
    return 1.0 / (picked + DAMPING), 1.0 / (e_in + DAMPING)


def split_body(bto_ref, bi_ref, out_ref):
    w_out, k_out = bto_ref.shape
    k_in = bi_ref.shape[0]
    rest = jnp.zeros((out_ref.shape[1] - w_out, k_out - k_in), bf16)
    for part, (b_out, b_in) in enumerate(zip(split2(bto_ref[...]), split2(bi_ref[...].T))):
        out_ref[part, :w_out, :] = b_out
        out_ref[part, w_out:, :k_in] = b_in
        out_ref[part, w_out:, k_in:] = rest


def rotate(rows, b_ref, w_out, k_out, k_in):
    n = rows.shape[0]
    w_pad = w_out + PAD
    lane = lax.broadcasted_iota(jnp.int32, (n, w_pad), 1)
    q_out, q_in = rows[:, :k_out], rows[:, k_out:]
    out = dot_nt(q_out, b_ref[0, :w_pad, :]) + dot_nt(q_out, b_ref[1, :w_pad, :])
    out = jnp.where(lane < w_out, out, 0.0)
    inn = dot_nt(q_in, b_ref[0, w_out:, :k_in]) + dot_nt(q_in, b_ref[1, w_out:, :k_in])
    s_out = level(jnp.max(jnp.abs(out), axis=1, keepdims=True))
    s_in = level(jnp.max(jnp.abs(inn), axis=1, keepdims=True))
    out = jnp.round(out * (1.0 / unit(s_out)))
    out = jnp.where(lane < w_out, out, jnp.where(lane < w_out + PAD // 2, s_out, s_in))
    inn = jnp.round(inn * (1.0 / unit(s_in)))
    return to_code(out), to_code(inn)


def rotate_own_body(
    n_out,
    n_in,
    w_out,
    at_ref,
    panel_ref,
    live_ref,
    eo_ref,
    ei_ref,
    q_ref,
    b_ref,
    rows_ref,
    code_ref,
    scale_ref,
    count_ref,
    wide,
):
    count_ref[...] = jnp.full(count_ref.shape, live_ref[0], jnp.int32)
    w_pad = w_out + PAD
    w_all = scale_ref.shape[1] // 2
    for k in range(2):
        s_out, s_in = panel_scales(at_ref[k], w_out, panel_ref, eo_ref, ei_ref)
        scale_ref[:, k * w_all : k * w_all + w_pad] = s_out
        scale_ref[:, k * w_all + w_pad : (k + 1) * w_all] = s_in
    n = q_ref.shape[0]
    wide[...] = q_ref[...].astype(f32).reshape(wide.shape)
    for r in range(n_out + n_in):
        rows_ref[:, r * LANES : (r + 1) * LANES] = wide[pl.ds(r, n, stride=SLOTS), :].astype(bf16)
    out, inn = rotate(rows_ref, b_ref, w_out, n_out * LANES, n_in * LANES)
    code_ref[:, : w_out + PAD] = out
    code_ref[:, w_out + PAD :] = inn


def rotate_mate_body(n_out, n_in, w_out, rows_ref, b_ref, code_ref, part_ref):
    out, inn = rotate(rows_ref, b_ref, w_out, n_out * LANES, n_in * LANES)
    w_all = code_ref.shape[1]
    for g in range(part_ref.shape[0]):
        part_ref[g, :, :w_all] = code_ref[...]
        part_ref[g, :, w_all : w_all + w_out + PAD] = out
        part_ref[g, :, w_all + w_out + PAD :] = inn


def back(both, b_hi, b_lo):
    n = both.shape[0] // 2
    x = dot_nn(both, b_hi)
    return x[:n] + x[n:] + dot_nn(both[:n], b_lo)


def restore_own_body(
    n_out, n_in, w_out, part_ref, scale_ref, own_ref, x_ref, mate_out_ref, mate_in_ref
):
    n = part_ref.shape[1]
    k_out, k_in = n_out * LANES, n_in * LANES
    w_in = own_ref.shape[1] - w_out
    w_pad = w_out + PAD
    w_all = w_pad + w_in
    lane = lax.broadcasted_iota(jnp.int32, (n, w_pad), 1)
    for k in range(2):
        at = k * w_all
        t_out = jnp.zeros((n, w_pad), f32)
        t_in = jnp.zeros((n, w_in), f32)
        for g in range(part_ref.shape[0]):
            x = from_code(part_ref[g, :, at : at + w_all])
            t_out += x[:, :w_pad] * unit(x[:, w_out : w_out + 1])
            t_in += x[:, w_pad:] * unit(x[:, w_out + PAD // 2 : w_out + PAD // 2 + 1])
        t_out = jnp.where(lane < w_out, t_out * scale_ref[:, at : at + w_pad], 0.0)
        t_in = t_in * scale_ref[:, at + w_pad : at + w_all]
        t_out = jnp.concatenate(split2(t_out), axis=0)
        t_in = jnp.concatenate(split2(t_in), axis=0)
        if k == 0:
            x_ref[:, :k_out] = back(t_out, own_ref[0, :w_pad, :], own_ref[1, :w_pad, :])
            x_ref[:, k_out:] = back(t_in, own_ref[0, w_out:, :k_in], own_ref[1, w_out:, :k_in])
        else:
            mate_out_ref[...] = t_out
            mate_in_ref[...] = t_in


def restore_mate_body(
    n_out, n_in, w_out, x_ref, mate_out_ref, mate_in_ref, mate_ref, code_ref, wide
):
    n = x_ref.shape[0]
    k_out, k_in = n_out * LANES, n_in * LANES
    w_pad = w_out + PAD
    x_out = x_ref[:, :k_out] + back(
        mate_out_ref[...], mate_ref[0, :w_pad, :], mate_ref[1, :w_pad, :]
    )
    x_in = x_ref[:, k_out:] + back(
        mate_in_ref[...], mate_ref[0, w_out:, :k_in], mate_ref[1, w_out:, :k_in]
    )
    for first, x, row in ((0, x_out, n_out + n_in), (n_out, x_in, n_out + n_in + 1)):
        steps = level(jnp.max(jnp.abs(x), axis=1, keepdims=True))
        codes = jnp.round(x * (1.0 / unit(steps)))
        for r in range(x.shape[1] // LANES):
            wide[pl.ds(first + r, n, stride=SLOTS), :] = codes[:, r * LANES : (r + 1) * LANES]
        wide[pl.ds(row, n, stride=SLOTS), :] = jnp.broadcast_to(steps, (n, LANES))
    code_ref[...] = to_code(wide[...]).reshape(code_ref.shape)


def sum_codes_body(n_out, n_in, code_ref, out_ref):
    slot = lax.broadcasted_iota(jnp.int32, (SLOTS, LANES), 0)
    is_out = slot < n_out
    is_in = jnp.logical_and(slot >= n_out, slot < n_out + n_in)
    total = jnp.zeros((SLOTS, LANES), f32)
    for j in range(code_ref.shape[0]):
        x = from_code(code_ref[j])
        a = x[n_out + n_in : n_out + n_in + 1]
        b = x[n_out + n_in + 1 : n_out + n_in + 2]
        total = total + x * jnp.where(is_out, unit(a), unit(b))
    size = jnp.abs(total)
    steps_out = level(jnp.max(jnp.where(is_out, size, 0.0), keepdims=True))
    steps_in = level(jnp.max(jnp.where(is_in, size, 0.0), keepdims=True))
    steps = jnp.where(is_out, steps_out, steps_in)
    codes = jnp.round(total * (1.0 / unit(steps)))
    codes = jnp.where(slot == n_out + n_in, steps_out, codes)
    codes = jnp.where(slot == n_out + n_in + 1, steps_in, codes)
    codes = to_code(codes)
    for j in range(out_ref.shape[0]):
        out_ref[j] = codes


def score_body(n_out, n_in, groups, count_ref, code_ref, to_ref, ti_ref, out_ref, wide):
    n = code_ref.shape[0] // groups
    rows = to_ref.shape[0]
    alongs = [jnp.zeros((2 * n, rows), f32)] * 2
    sides = ((0, n_out, to_ref), (n_out, n_in, ti_ref))
    for g in range(groups):
        wide[...] = from_code(code_ref[g * n : (g + 1) * n]).reshape(wide.shape)

        def row(r):
            return wide[pl.ds(r, n, stride=SLOTS), :]

        for side, (first, count, t_ref) in enumerate(sides):
            scale = unit(row(n_out + n_in + side))
            scale = jnp.concatenate([scale, scale], axis=1)
            for r in range(0, count, 2):
                pair = jnp.concatenate([row(first + r), row(first + r + 1)], axis=1)
                both = jnp.concatenate(split2(pair * scale), axis=0)
                at = (g * count + r) * LANES
                alongs[side] += dot_nt(both, t_ref[:, at : at + 2 * LANES])
    along_out, along_in = alongs
    product = (along_out[:n] + along_out[n:]) * (along_in[:n] + along_in[n:])
    span = 16 // NQ
    by_query = []
    for q in range(NQ):
        total = product[q * span : (q + 1) * span]
        for first in range((q + NQ) * span, n, NQ * span):
            total = total + product[first : first + span]
        by_query.append(jnp.sum(total, axis=0, keepdims=True))
    s_id = lax.broadcasted_iota(jnp.int32, (1, rows), 1) // RANK
    row = lax.broadcasted_iota(jnp.int32, out_ref.shape, 0)
    col = lax.broadcasted_iota(jnp.int32, out_ref.shape, 1)
    result = jnp.zeros(out_ref.shape, f32)
    for s in range(SEQ_DEV):
        for q in range(NQ):
            picked = jnp.where(s_id == s, by_query[q], 0.0)
            value = jnp.sum(picked, axis=1, keepdims=True) * (1.0 / RANK)
            result = jnp.where(jnp.logical_and(row == s, col == q), value, result)
    out_ref[...] = jnp.where(row < count_ref[:, :NQ], result, 0.0)


def spread(x, axes):
    n = lax.axis_size(axes)
    x = jnp.broadcast_to(x[None], (n, *x.shape))
    return lax.all_to_all(x, axes, split_axis=0, concat_axis=0, tiled=True)


def per_device(qo, qi, bo, bi, eo, ei, panels, to, ti, live):
    n_out, n_in = qo.shape[1] // LANES, qi.shape[1] // LANES
    data = n_out + n_in
    nz, nxl, nc = (lax.axis_size(a) for a in BLK)
    n_grp = lax.axis_size(GRP)
    half = nz * nxl
    n_rows = half * nc
    position = lax.axis_index(BLK)
    w_out, w_in = bo.shape[1], bi.shape[1]
    w_all = w_out + PAD + w_in

    own_q = jnp.concatenate([qo, qi], axis=1).reshape(data, LANES)
    own_q = jnp.pad(own_q, ((0, SLOTS - data), (0, 0)))
    queries = spread(own_q, ("z", "xl"))

    mate_spot = position + 1 - 2 * lax.axis_index("c")
    spots = jnp.stack([position, mate_spot]).astype(jnp.int32)
    own = call(
        split_body, jax.ShapeDtypeStruct((2, w_out + w_in, bo.shape[0]), bf16), n_in=2
    )(bo.T, bi)
    mate = lax.ppermute(own, "c", [(0, 1), (1, 0)])
    rows, own_part, scale, count = call(
        functools.partial(rotate_own_body, n_out, n_in, w_out),
        (
            jax.ShapeDtypeStruct((half, data * LANES), bf16),
            jax.ShapeDtypeStruct((half, w_all), jnp.int16),
            jax.ShapeDtypeStruct((1, nc * w_all), f32),
            jax.ShapeDtypeStruct((SEQ_DEV, LANES), jnp.int32),
        ),
        [pltpu.VMEM((half * SLOTS, LANES), f32)],
        n_in=7,
        smem=(0, 1, 2),
        flops=OWN_FLOPS,
    )(spots, panels, live, eo.reshape(-1, LANES), ei.reshape(-1, w_in), queries, own)
    part = call(
        functools.partial(rotate_mate_body, n_out, n_in, w_out),
        jax.ShapeDtypeStruct((n_grp, half, nc * w_all), jnp.int16),
        n_in=3,
    )(rows, mate, own_part)
    parts = lax.all_to_all(part, GRP, split_axis=0, concat_axis=0, tiled=True)

    x_own, mate_out, mate_in = call(
        functools.partial(restore_own_body, n_out, n_in, w_out),
        (
            jax.ShapeDtypeStruct((half, data * LANES), f32),
            jax.ShapeDtypeStruct((2 * half, w_out + PAD), bf16),
            jax.ShapeDtypeStruct((2 * half, w_in), bf16),
        ),
        n_in=3,
        flops=OWN_FLOPS,
    )(parts, scale, own)
    codes = call(
        functools.partial(restore_mate_body, n_out, n_in, w_out),
        jax.ShapeDtypeStruct((half, SLOTS, LANES), jnp.int16),
        [pltpu.VMEM((half * SLOTS, LANES), f32)],
        n_in=4,
    )(x_own, mate_out, mate_in, mate)
    codes = lax.all_to_all(codes, ("z", "xl"), split_axis=0, concat_axis=0, tiled=True)
    codes = call(
        functools.partial(sum_codes_body, n_out, n_in),
        jax.ShapeDtypeStruct((nz, SLOTS, LANES), jnp.int16),
    )(codes)
    codes = lax.all_to_all(codes, "z", split_axis=0, concat_axis=0, tiled=True)
    codes = lax.all_gather(codes, ("y", "xh", "xl", "c"), axis=0, tiled=True)
    return call(
        functools.partial(score_body, n_out, n_in, n_grp),
        jax.ShapeDtypeStruct((SEQ_DEV, NQ), f32),
        [
            pltpu.VMEM((n_rows * SLOTS, LANES), f32),
        ],
        n_in=4,
    )(count, codes, to, ti)


def solution(mesh):
    fine = Mesh(mesh.devices.reshape(4, 2, 16, 2, 2), GRP + BLK)
    in_specs = (
        P(BLK, GRP),
        P(BLK, GRP),
        P(GRP, BLK),
        P(GRP, BLK),
        P(),
        P(),
        P(),
        P(GRP + BLK, None),
        P(GRP + BLK, None),
        P(GRP + BLK),
    )
    out_specs = P(GRP + BLK, None)
    return jax.shard_map(
        per_device, mesh=fine, in_specs=in_specs, out_specs=out_specs, check_vma=False
    )
```
